256 devices in a mesh: replica: 8 (over y_lo, x), fsdp: 32 (over z, y_hi, core).
Axes of the slice: x: 4, y: 4 (y_hi: 2, y_lo: 2; y = y_hi * 2 + y_lo), z: 8, core: 2. Of those that a mesh axis runs over, the one named last changes fastest.
Arguments:
- embedded: bfloat16 [8, 12288, 8192], P('replica', 'fsdp'), may hold values from -6 to 6
- positions: int32 [8, 12288], P('replica', 'fsdp'), may hold values from 0 to 8191
- key_cotangent: bfloat16 [8, 12288, 512], P('replica', 'fsdp'), may hold values from -0.125 to 0.125
- local_weight: float32 [8, 8192, 512], P('replica', 'fsdp'), may hold values from -0.0625 to 0.0625
- adam_first: float32 [8, 8192, 512], P('replica', 'fsdp'), may hold values from -6 to 6
- adam_second: float32 [8, 8192, 512], P('replica', 'fsdp'), may hold values from 0.01 to 1
- pseudo_grad: float32 [8, 8192, 512], P('replica', 'fsdp'), may hold values from -0.00061035156 to 0.00061035156
- anchor: float32 [8192, 512], P('fsdp'), may hold values from -0.0625 to 0.0625
- momentum: float32 [8192, 512], P('fsdp'), may hold values from -0.00061035156 to 0.00061035156
Outputs:
- keys: bfloat16 [8, 12288, 512], P('replica', 'fsdp')
- merged: float32 [8, 8192, 512], P('replica', 'fsdp')
- new_first: float32 [8, 8192, 512], P('replica', 'fsdp')
- new_second: float32 [8, 8192, 512], P('replica', 'fsdp')
- new_anchor: float32 [8192, 512], P('fsdp')
- new_momentum: float32 [8192, 512], P('fsdp')
The draws below stay inside these ranges and needn't reach their ends.
All inputs are finite; a program needn't handle non-finite values.
Results may differ from the reference program's by a relative error of at most 0.0065.
Values may be sent and summed in bfloat16 or wider, within the bound.
A program may use at most 128 MiB of HBM per device.

```python
import math
import jax
import jax.numpy as jnp
from jax import lax

D = 8192
HD = 128
KV_HEADS = 4
TOK_DEV = 384
KW = 512
TOKREP = 12288
N_REPLICA = 8
N_FSDP = 32


def plant(drawn, stream_key, least, largest):
    dims = drawn.shape
    index_at = [jax.random.randint(jax.random.fold_in(stream_key, axis), (), 0, dims[axis]) for axis in range(len(dims))]
    drawn = drawn.at[tuple(index_at)].set(least)
    longest = dims.index(max(dims))
    index_at[longest] = (index_at[longest] + 1) % dims[longest]
    return drawn.at[tuple(index_at)].set(largest)


def raised(drawn, stream_key, source, target, shards_of, factor):
    owner, partner = [(jnp.arange(drawn.shape[position]) // (drawn.shape[position] // shards_of)).reshape([-1 if axis == position else 1 for axis in range(drawn.ndim)]) for position in (source, target)]
    chosen = jax.random.permutation(stream_key, shards_of)[partner]
    strong = (owner == chosen) | (owner == (partner + shards_of // 2) % shards_of)
    return jnp.where(strong, factor * drawn, drawn)


def block_levels(stream_key, dims, pieces, least, top_value):
    factor_of, own = 1.0, jax.random.fold_in(stream_key, 6)
    for axis_at, parts in pieces:
        draws = jnp.exp(jax.random.uniform(jax.random.fold_in(own, axis_at), (parts,), jnp.float32, least / len(pieces), top_value / len(pieces)))
        factor_of = factor_of * jnp.repeat(draws, dims[axis_at] // parts).reshape([-1 if axis == axis_at else 1 for axis in range(len(dims))])
    return factor_of


def gaussian(stream_key, shape, width, bound, split=(), held_as=jnp.bfloat16):
    result = jax.random.normal(stream_key, shape, jnp.float32) * width
    if len(split) > 0:
        result = block_levels(stream_key, shape, split, -0.22, 0.18) * result
    return jnp.clip(result, min=-bound, max=bound).astype(held_as)


def bell_draw_with(stream_key, shape, spread, limit, cuts, heavy, held_as=jnp.bfloat16):
    result = spread * jax.random.normal(stream_key, shape, jnp.float32)
    if cuts:
        result = result * block_levels(stream_key, shape, cuts, -0.22, 0.18)
    return jnp.clip(raised(result, jax.random.fold_in(stream_key, 3), *heavy), -limit, limit).astype(held_as)


def setup_inputs(seed: int = 0) -> dict:
    splits = jax.random.split(jax.random.key(seed), 10)
    return {
        "embedded": bell_draw_with(splits[0], (N_REPLICA, TOKREP, D), 1.0, 6.0, ((0, 8), (1, 32)), (1, 2, 32, 2.75)),
        "positions": plant(jax.random.randint(splits[1], (N_REPLICA, TOKREP), 0, 8192), jax.random.fold_in(splits[1], 1), 0, 8191).astype(jnp.int32),
        "key_cotangent": gaussian(splits[2], (N_REPLICA, TOKREP, KW), ((TOK_DEV * N_FSDP) ** -0.5), 0.125, ((0, 8), (1, 32))),
        "local_weight": gaussian(splits[3], (N_REPLICA, D, KW), D ** -0.5, 0.0625, ((0, 8), (1, 32)), jnp.float32),
        "adam_first": gaussian(splits[4], (N_REPLICA, D, KW), 1.0, 6.0, ((0, 8), (1, 32)), jnp.float32),
        "adam_second": jnp.clip(jnp.exp(math.log(1.0) - 4.6051702 * jax.random.uniform(splits[5], (N_REPLICA, D, KW), jnp.float32) ** block_levels(splits[5], (N_REPLICA, D, KW), ((0, 8), (1, 32)), -0.2, 0.2)), 0.01, 1.0),
        "pseudo_grad": gaussian(splits[6], (N_REPLICA, D, KW), (0.01 * D ** -0.5), 0.00061035156, ((0, 8), (1, 32)), jnp.float32),
        "anchor": gaussian(splits[7], (D, KW), D ** -0.5, 0.0625, ((0, 32),), jnp.float32),
        "momentum": gaussian(splits[8], (D, KW), (0.01 * D ** -0.5), 0.00061035156, ((0, 32),), jnp.float32),
    }


def rope_tables(positions, size):
    half = size // 2
    steps = jnp.arange(half).astype(jnp.float32)
    freqs = jnp.exp(steps * (-2.0 * math.log(500000.0) / size))
    angle = positions.astype(jnp.float32)[:, None] * freqs[None, :]
    return (jnp.cos(angle)[:, None, :], jnp.sin(angle)[:, None, :])

def rotate_keys(plain, cosine, sine, heads, size):
    count = plain.shape[0]
    half = size // 2
    shaped = plain.reshape(count, heads, size)
    first = shaped[:, :, :half]
    second = shaped[:, :, half:]
    out = jnp.concatenate([first * cosine - second * sine, second * cosine + first * sine], axis=2)
    return out.reshape(count, heads * size)

def unrotate_grad(upper, cosine, sine, heads, size):
    count = upper.shape[0]
    half = size // 2
    shaped = upper.astype(jnp.float32).reshape(count, heads, size)
    first = shaped[:, :, :half]
    second = shaped[:, :, half:]
    out = jnp.concatenate([first * cosine + second * sine, second * cosine - first * sine], axis=2)
    return out.reshape(count, heads * size)

def reference(embedded, positions, key_cotangent, local_weight, adam_first, adam_second, pseudo_grad, anchor, momentum):
    mean_delta = lax.optimization_barrier(jnp.sum(pseudo_grad, axis=0)) / N_REPLICA
    new_momentum = 0.9 * momentum + mean_delta
    new_anchor = anchor - 0.7 * (mean_delta + 0.9 * new_momentum)
    keys_all = []
    merged_all = []
    first_all = []
    second_all = []
    for index in range(N_REPLICA):
        inputs = embedded[index]
        weight_b = local_weight[index].astype(jnp.bfloat16)
        cosine, sine = rope_tables(positions[index], HD)
        plain = jnp.dot(inputs, weight_b, preferred_element_type=jnp.float32)
        keys_all.append(rotate_keys(plain, cosine, sine, KV_HEADS, HD).astype(jnp.bfloat16))
        key_grad = unrotate_grad(key_cotangent[index], cosine, sine, KV_HEADS, HD).astype(jnp.bfloat16)
        grad = lax.dot_general(inputs, key_grad, (((0,), (0,)), ((), ())), preferred_element_type=jnp.float32)
        first = 0.9 * adam_first[index] + 0.1 * grad
        second = 0.999 * adam_second[index] + 0.001 * grad * grad
        weight = local_weight[index]
        stepped = weight - 0.001 * (first / (jnp.sqrt(second) + 1e-08) + 0.1 * weight)
        merged_all.append(0.5 * new_anchor + 0.5 * stepped)
        first_all.append(first)
        second_all.append(second)
    return (jnp.stack(keys_all), jnp.stack(merged_all), jnp.stack(first_all), jnp.stack(second_all), new_anchor, new_momentum)
```

```python
import functools
import math

import jax
import jax.numpy as jnp
import numpy as np
from jax import lax
from jax.experimental import pallas as pl
from jax.experimental.pallas import tpu as pltpu
from jax.sharding import PartitionSpec as P

HD = 128
KV_HEADS = 4
NZ = 8
NX = 4
TOK = 384
ROWS = 256
KW = 512
HALF = 256
MESH = pl.DeviceIdType.MESH
F32 = jnp.float32
BF16 = jnp.bfloat16


def frequencies():
    steps = np.arange(HD // 2, dtype=np.float64)
    freqs = np.exp(steps * (-2.0 * math.log(500000.0) / HD)).astype(np.float32)
    return np.concatenate([freqs, freqs])[None, :]


def kernel(
    emb, pos, freq, cot, weight, pseudo,
    keys_out, grad_out, delta_out,
    emba, wall, wf, cotv, psv, psb, kgt, ysend, yrecv, own, zs, zr, acc, accx,
    cosv, sinv, keyv, gout, p1, p2s, p2r, dsum,
    loc, embl, embs, embr, kgs, kgr, ags, agr, yas, yar, yss, yrr, zss, zrr, xs, xr, p1ss, p1rr, p2ss, p2rr, p3ss, p3rr, outs,
):
    r = lax.axis_index("replica")
    f = lax.axis_index("fsdp")
    ylo, x = r // NX, r % NX
    z, yh, c = f // 4, (f // 2) % 2, f % 2

    def wrap(v):
        return lax.rem(v + 2 * NZ, NZ)

    def at_z(v):
        return (r, wrap(v) * 4 + yh * 2 + c)

    nexts = (at_z(z + 1), at_z(z - 1))
    across = (r, z * 4 + (1 - yh) * 2 + c)
    twin = (r, z * 4 + yh * 2 + (1 - c))
    xpeers = [(ylo * NX + lax.rem(x + k, NX), f) for k in (1, 2, 3)]
    ypeer = ((1 - ylo) * NX + x, f)

    def remote(src, dst, ss, rs, dev):
        return pltpu.make_async_remote_copy(
            src_ref=src, dst_ref=dst, send_sem=ss, recv_sem=rs, device_id=dev, device_id_type=MESH
        )

    def slot(zz, plane):
        return wrap(zz) * 2 + plane

    def place(j):
        i = j % 8
        away = (4 - (i + 1) // 2) * (2 * (i % 2) - 1)
        return slot(z + away, jnp.where(j < 8, 1 - yh, yh))

    load_w = pltpu.make_async_copy(weight, wf, loc.at[0])
    load_c = pltpu.make_async_copy(cot, cotv, loc.at[1])
    load_p = pltpu.make_async_copy(pseudo, psv, loc.at[2])

    def load_emb(j):
        b = place(j)
        cols = pl.multiple_of((2 * b + c) * ROWS, ROWS)
        return pltpu.make_async_copy(emb.at[:, pl.ds(cols, ROWS)], emba.at[b, pl.ds(0, TOK)], embl.at[j])

    def swap_emb(j):
        b = place(j)
        cols = pl.multiple_of((2 * b + 1 - c) * ROWS, ROWS)
        return remote(
            emb.at[:, pl.ds(cols, ROWS)], emba.at[b, pl.ds(TOK, TOK)], embs.at[j], embr.at[j], twin
        )

    load_w.start()
    load_c.start()
    load_p.start()
    lax.fori_loop(0, 16, lambda j, _: (load_emb(j).start(), 0)[1], 0)

    barrier = pltpu.get_barrier_semaphore()
    friends = [*nexts, across, twin, *xpeers, ypeer]
    for dev in friends:
        pl.semaphore_signal(barrier, inc=1, device_id=dev, device_id_type=MESH)

    load_w.wait()
    mine = slot(z, yh)
    other = slot(z, 1 - yh)
    wall[mine] = wf[...].astype(BF16)
    pl.semaphore_wait(barrier, len(friends))

    def ring(way, k):
        d, p = k // 2, k % 2
        sign = 1 if way == 0 else -1
        b = slot(z - sign * d, yh if p == 0 else 1 - yh)
        if d < 3:
            ref = wall.at[b]
        else:
            ref = wall.at[b, pl.ds(way * (ROWS // 2), ROWS // 2)]
        return remote(ref, ref, ags.at[way, k], agr.at[way, k], nexts[way])

    def ring_in(way, k):
        d, p = k // 2, k % 2
        sign = 1 if way == 0 else -1
        b = slot(z - sign * (d + 1), yh if p == 0 else 1 - yh)
        if d < 3:
            ref = wall.at[b]
        else:
            ref = wall.at[b, pl.ds(way * (ROWS // 2), ROWS // 2)]
        return remote(ref, ref, ags.at[way, k], agr.at[way, k], nexts[way])

    ring(0, 0).start()
    ring(1, 0).start()
    cross = remote(wall.at[mine], wall.at[mine], yas.at[0], yar.at[0], across)
    cross_in = remote(wall.at[other], wall.at[other], yas.at[0], yar.at[0], across)
    cross.start()
    lax.fori_loop(0, 16, lambda j, _: (swap_emb(j).start(), 0)[1], 0)

    posf = pos[...].astype(F32)
    cols = [
        jnp.transpose(jnp.broadcast_to(posf[:, 128 * j : 128 * (j + 1)], (128, 128))) for j in range(3)
    ]
    lane = lax.broadcasted_iota(jnp.int32, (192, 128), 1)
    low = lane < HD // 2
    lower = jnp.concatenate([cols[0], cols[1][:64]], axis=0)
    upper = jnp.concatenate([cols[1][64:], cols[2]], axis=0)
    angle = jnp.where(low, lower, upper) * freq[...]
    cp, sp = jnp.cos(angle), jnp.sin(angle)
    cq, sq = pltpu.roll(cp, 64, 1), pltpu.roll(sp, 64, 1)
    cosv[0:192, :] = jnp.where(low, cp, cq)
    cosv[192:384, :] = jnp.where(low, cq, cp)
    sinv[0:192, :] = jnp.where(low, -sp, sq)
    sinv[192:384, :] = jnp.where(low, -sq, sp)

    load_c.wait()
    for h in range(KV_HEADS):
        u = cotv[:, h * HD : (h + 1) * HD].astype(F32)
        g = u * cosv[...] - pltpu.roll(u, 64, 1) * sinv[...]
        kgt[h * HD : (h + 1) * HD, 0:TOK] = jnp.transpose(g).astype(BF16)
    give_kg = remote(kgt.at[:, pl.ds(0, TOK)], kgt.at[:, pl.ds(TOK, TOK)], kgs.at[0], kgr.at[0], twin)
    give_kg.start()

    load_p.wait()
    psb[...] = psv[...].astype(BF16)

    def piece(xx):
        return pl.ds(pl.multiple_of(xx * 64, 64), 64)

    stage1 = [
        remote(psb.at[piece(lax.rem(x + k, NX))], p1.at[k - 1], p1ss.at[k - 1], p1rr.at[k - 1], xpeers[k - 1])
        for k in (1, 2, 3)
    ]
    for cp1 in stage1:
        cp1.start()

    def block(j):
        load_emb(j).wait()
        swap_emb(j).wait_recv()
        return jnp.dot(kgt[...], emba[place(j)], preferred_element_type=F32)

    def send_y(i):
        return remote(ysend.at[i], yrecv.at[i], yss.at[i], yrr.at[i], across)

    def far(i, send):
        ysend[i] = block(i).astype(BF16)
        if send:
            send_y(i).start()
        return 0

    def near(i, _):
        own[i] = block(i + 8)
        return 0

    give_kg.wait_recv()
    lax.fori_loop(0, 3, lambda i, _: far(i, True), 0)

    cross_in.wait_recv()
    ring(0, 1).start()
    ring(1, 1).start()

    lax.fori_loop(3, 8, lambda i, _: far(i, False), 0)

    def advance(k):
        for way in (0, 1):
            ring_in(way, k).wait_recv()
            if k + 2 < 8:
                ring(way, k + 2).start()

    advance(0)
    lax.fori_loop(0, 8, near, 0)

    def product(b, first=False):
        def part(m, _):
            at = pl.ds(pl.multiple_of(m * 256, 256), 256)
            value = jnp.dot(emba[b, at, :], wall[b], preferred_element_type=F32)
            if first:
                acc[at, :] = value
            else:
                acc[at, :] += value
            return 0

        lax.fori_loop(0, 3, part, 0)

    def products(k):
        d, p = k // 2, k % 2
        plane = yh if p == 0 else 1 - yh
        product(slot(z - d - 1, plane))
        if d < 3:
            product(slot(z + d + 1, plane))

    product(mine, True)
    product(other)

    for cp1 in stage1:
        cp1.wait_recv()
    part_sum = psb[piece(x), :].astype(F32)
    for k in range(3):
        part_sum = part_sum + p1[k].astype(F32)
    p2s[...] = part_sum.astype(BF16)
    stage2 = remote(p2s, p2r, p2ss.at[0], p2rr.at[0], ypeer)
    stage2.start()

    def next_y(i):
        send_y(i - 3).wait_send()
        send_y(i).start()

    def hand(way, step, h):
        rows = pl.ds(h * HALF, HALF)
        return remote(
            zs.at[way, step, rows], zr.at[way, step, rows],
            zss.at[way, step * 2 + h], zrr.at[way, step * 2 + h], nexts[way],
        )

    def here(i, h):
        rows = pl.ds(h * HALF, HALF)
        return own[i, rows, :] + yrecv[i, rows, :].astype(F32)

    def relay(i, way, step):
        send_y(i).wait_recv()
        halves = (1, 0) if way == 0 else (0, 1)
        for h in halves:
            rows = pl.ds(h * HALF, HALF)
            total = here(i, h)
            if step > 1 or h == way:
                hand(way, step - 1, h).wait_recv()
                total = total + zr[way, step - 1, rows, :].astype(F32)
            zs[way, step, rows, :] = total.astype(BF16)
            hand(way, step, h).start()

    next_y(3)
    send_y(0).wait_recv()
    for way in (0, 1):
        rows = pl.ds(way * HALF, HALF)
        zs[way, 0, rows, :] = here(0, way).astype(BF16)
        hand(way, 0, way).start()
    advance(1)
    products(0)
    products(1)
    next_y(4)
    relay(1, 0, 1)

    stage2.wait_recv()
    dsum[piece(x), :] = (p2s[...].astype(F32) + p2r[...].astype(F32)).astype(BF16)
    stage3 = [
        remote(dsum.at[piece(x)], dsum.at[piece(x)], p3ss.at[k - 1], p3rr.at[k - 1], xpeers[k - 1])
        for k in (1, 2, 3)
    ]
    stage3_in = [
        remote(
            dsum.at[piece(lax.rem(x + NX - k, NX))], dsum.at[piece(lax.rem(x + NX - k, NX))],
            p3ss.at[k - 1], p3rr.at[k - 1], xpeers[k - 1],
        )
        for k in (1, 2, 3)
    ]
    for cp3 in stage3:
        cp3.start()

    advance(2)
    products(2)
    next_y(5)
    relay(2, 1, 1)
    advance(3)
    products(3)
    next_y(6)
    relay(3, 0, 2)
    for cp3 in stage3_in:
        cp3.wait_recv()
    save_d = pltpu.make_async_copy(dsum, delta_out, outs.at[0])
    save_d.start()
    advance(4)
    products(4)
    next_y(7)
    relay(4, 1, 2)
    advance(5)
    products(5)
    relay(5, 0, 3)
    advance(6)
    products(6)
    relay(6, 1, 3)
    advance(7)
    products(7)

    give_x = remote(acc.at[pl.ds(TOK, TOK)], accx, xs.at[0], xr.at[0], twin)
    give_x.start()
    give_x.wait_recv()
    for h in range(KV_HEADS):
        at = slice(h * HD, (h + 1) * HD)
        plain = acc[0:TOK, at] + accx[:, at]
        keyv[:, at] = (plain * cosv[...] + pltpu.roll(plain, 64, 1) * sinv[...]).astype(BF16)
    save_k = pltpu.make_async_copy(keyv, keys_out, outs.at[1])
    save_k.start()

    send_y(7).wait_recv()
    for h in (0, 1):
        rows = pl.ds(h * HALF, HALF)
        total = here(7, h)
        for way in (0, 1):
            hand(way, 3, h).wait_recv()
            total = total + zr[way, 3, rows, :].astype(F32)
        gout[:, h * HALF : (h + 1) * HALF] = jnp.transpose(total)
    save_g = pltpu.make_async_copy(gout, grad_out, outs.at[2])
    save_g.start()

    for k in range(8):
        for way in (0, 1):
            ring(way, k).wait_send()
    cross.wait_send()
    lax.fori_loop(0, 16, lambda j, _: (swap_emb(j).wait_send(), 0)[1], 0)
    give_kg.wait_send()
    give_x.wait_send()
    for i in (5, 6, 7):
        send_y(i).wait_send()
    for way in (0, 1):
        for step in range(4):
            for h in (0, 1):
                if step > 0 or h == way:
                    hand(way, step, h).wait_send()
    for cp in [*stage1, stage2, *stage3]:
        cp.wait_send()
    save_d.wait()
    save_k.wait()
    save_g.wait()


def step(embedded, positions, cotangent, weight, pseudo):
    any_spec = pl.BlockSpec(memory_space=pl.ANY)
    vmem_spec = pl.BlockSpec(memory_space=pltpu.VMEM)
    dma = pltpu.SemaphoreType.DMA
    return pl.pallas_call(
        kernel,
        out_shape=(
            jax.ShapeDtypeStruct((TOK, KW), BF16),
            jax.ShapeDtypeStruct((ROWS, KW), F32),
            jax.ShapeDtypeStruct((ROWS, KW), BF16),
        ),
        in_specs=[any_spec, vmem_spec, vmem_spec, any_spec, any_spec, any_spec],
        out_specs=(any_spec, any_spec, any_spec),
        scratch_shapes=[
            pltpu.VMEM((16, 2 * TOK, ROWS), BF16),
            pltpu.VMEM((16, ROWS, KW), BF16),
            pltpu.VMEM((ROWS, KW), F32),
            pltpu.VMEM((TOK, KW), BF16),
            pltpu.VMEM((ROWS, KW), F32),
            pltpu.VMEM((ROWS, KW), BF16),
            pltpu.VMEM((KW, 2 * TOK), BF16),
            pltpu.VMEM((8, KW, ROWS), BF16),
            pltpu.VMEM((8, KW, ROWS), BF16),
            pltpu.VMEM((8, KW, ROWS), F32),
            pltpu.VMEM((2, 4, KW, ROWS), BF16),
            pltpu.VMEM((2, 4, KW, ROWS), BF16),
            pltpu.VMEM((2 * TOK, KW), F32),
            pltpu.VMEM((TOK, KW), F32),
            pltpu.VMEM((TOK, HD), F32),
            pltpu.VMEM((TOK, HD), F32),
            pltpu.VMEM((TOK, KW), BF16),
            pltpu.VMEM((ROWS, KW), F32),
            pltpu.VMEM((3, 64, KW), BF16),
            pltpu.VMEM((64, KW), BF16),
            pltpu.VMEM((64, KW), BF16),
            pltpu.VMEM((ROWS, KW), BF16),
            dma((3,)),
            dma((16,)),
            dma((16,)),
            dma((16,)),
            dma((1,)),
            dma((1,)),
            dma((2, 8)),
            dma((2, 8)),
            dma((1,)),
            dma((1,)),
            dma((8,)),
            dma((8,)),
            dma((2, 8)),
            dma((2, 8)),
            dma((1,)),
            dma((1,)),
            dma((3,)),
            dma((3,)),
            dma((1,)),
            dma((1,)),
            dma((3,)),
            dma((3,)),
            dma((3,)),
        ],
        compiler_params=pltpu.CompilerParams(
            collective_id=0, has_side_effects=True, vmem_limit_bytes=48 * 1024 * 1024
        ),
        cost_estimate=pl.CostEstimate(flops=6442450944, bytes_accessed=10 << 20, transcendentals=0),
    )(embedded, positions, jnp.asarray(frequencies()), cotangent, weight, pseudo)


def outer_update(delta_sum, count, anchor_rows, momentum_rows):
    mean_delta = delta_sum / count
    momentum_next = 0.9 * momentum_rows + mean_delta
    anchor_next = anchor_rows - 0.7 * (mean_delta + 0.9 * momentum_next)
    return (anchor_next, momentum_next)


def local(
    embedded,
    positions,
    key_cotangent,
    local_weight,
    adam_first,
    adam_second,
    pseudo_grad,
    anchor,
    momentum,
):
    weight = local_weight[0]
    keys, grad, delta = step(embedded[0], positions, key_cotangent[0], weight, pseudo_grad[0])
    first = 0.9 * adam_first[0] + 0.1 * grad
    second = 0.999 * adam_second[0] + 0.001 * grad * grad
    stepped = weight - 0.001 * (first / (jnp.sqrt(second) + 1e-08) + 0.1 * weight)
    replicas = lax.axis_size("replica")
    anchor_next, momentum_next = outer_update(delta.astype(F32), replicas, anchor, momentum)
    merged = 0.5 * anchor_next + 0.5 * stepped
    return (keys[None], merged[None], first[None], second[None], anchor_next, momentum_next)


def solution(mesh):
    return jax.shard_map(
        local,
        mesh=mesh,
        in_specs=(
            P("replica", "fsdp", None),
            P("replica", "fsdp"),
            P("replica", "fsdp", None),
            P("replica", "fsdp", None),
            P("replica", "fsdp", None),
            P("replica", "fsdp", None),
            P("replica", "fsdp", None),
            P("fsdp", None),
            P("fsdp", None),
        ),
        out_specs=(
            P("replica", "fsdp", None),
            P("replica", "fsdp", None),
            P("replica", "fsdp", None),
            P("replica", "fsdp", None),
            P("fsdp", None),
            P("fsdp", None),
        ),
        check_vma=False,
    )
```

```python
import functools
import math

import jax
import jax.numpy as jnp
import numpy as np
from jax import lax
from jax.experimental import pallas as pl
from jax.experimental.pallas import tpu as pltpu
from jax.sharding import PartitionSpec as P

HD = 128
KV_HEADS = 4
NZ = 8
NX = 4
TOK = 384
ROWS = 256
KW = 512
HALF = 256
HOP = 64
AHEAD = 2
MESH = pl.DeviceIdType.MESH
F32 = jnp.float32
BF16 = jnp.bfloat16


def frequencies():
    steps = np.arange(HD // 2, dtype=np.float64)
    freqs = np.exp(steps * (-2.0 * math.log(500000.0) / HD)).astype(np.float32)
    return np.concatenate([freqs, freqs])[None, :]


def kernel(
    emb, pos_in, freq_in, cot, weight, pseudo,
    keyv, gout, dsum,
    emba, wall, wf, cotv, psv, psb, kgt, ysend, yrecv, own, zs, zr, acc, accx,
    cosv, sinv, p1, p2s, p2r, pos, freq,
    loc, embl, embs, embr, kgs, kgr, ags, agr, yas, yar, yss, yrr, zss, zrr, xs, xr, p1ss, p1rr, p2ss, p2rr, p3ss, p3rr,
):
    r = lax.axis_index("replica")
    f = lax.axis_index("fsdp")
    ylo, x = r // NX, r % NX
    z, yh, c = f // 4, (f // 2) % 2, f % 2

    def wrap(v):
        return lax.rem(v + 2 * NZ, NZ)

    def at_z(v):
        return (r, wrap(v) * 4 + yh * 2 + c)

    nexts = (at_z(z + 1), at_z(z - 1))
    across = (r, z * 4 + (1 - yh) * 2 + c)
    twin = (r, z * 4 + yh * 2 + (1 - c))
    xpeers = [(ylo * NX + lax.rem(x + k, NX), f) for k in (1, 2, 3)]
    ypeer = ((1 - ylo) * NX + x, f)

    def remote(src, dst, ss, rs, dev):
        return pltpu.make_async_remote_copy(
            src_ref=src, dst_ref=dst, send_sem=ss, recv_sem=rs, device_id=dev, device_id_type=MESH
        )

    def slot(zz, plane):
        return wrap(zz) * 2 + plane

    def place(j):
        i = j % 8
        away = (4 - (i + 1) // 2) * (2 * (i % 2) - 1)
        return slot(z + away, jnp.where(j < 8, 1 - yh, yh))

    load_w = [
        pltpu.make_async_copy(weight.at[pl.ds(h * 128, 128)], wf.at[pl.ds(h * 128, 128)], loc.at[h]) for h in (0, 1)
    ]
    load_t = pltpu.make_async_copy(pos_in, pos.at[0], loc.at[2])
    load_f = pltpu.make_async_copy(freq_in, freq, loc.at[3])
    load_c = pltpu.make_async_copy(cot, cotv.at[0], loc.at[4])
    load_p = pltpu.make_async_copy(pseudo, psv, loc.at[5])
    load_w[0].start()
    load_w[1].start()
    barrier = pltpu.get_barrier_semaphore()
    friends = [*nexts, across, twin, *xpeers, ypeer]
    for dev in friends:
        pl.semaphore_signal(barrier, inc=1, device_id=dev, device_id_type=MESH)
    load_t.start()
    load_f.start()
    load_c.start()

    mine, other = slot(z, yh), slot(z, 1 - yh)

    def rows_of(k, h):
        if k == 1 and h == 1:
            return pl.ds(128, 128 - HOP)
        return pl.ds(h * 128, 128)

    def travels(way, k, h):
        return h == way if k >= 6 else not (k == 1 and h == 1 and HOP == 128)

    def ring(way, k, h, back=0):
        sign = 1 if way == 0 else -1
        b = slot(z - sign * (k // 2 + back), yh if k % 2 == 0 else 1 - yh)
        ref = wall.at[b, rows_of(k, h)]
        return remote(ref, ref, ags.at[way, k * 2 + h], agr.at[way, k * 2 + h], nexts[way])

    def ring_in(way, k, h):
        return ring(way, k, h, 1)

    def cross(h, b):
        ref = wall.at[b, pl.ds(h * 128, 128)]
        return remote(ref, ref, yas.at[h], yar.at[h], across)

    def hop(way, plane):
        ref = wall.at[slot(z - (1 if way == 0 else -1), plane), pl.ds(ROWS - HOP, HOP)]
        return remote(ref, ref, yas.at[2 + way], yar.at[2 + way], across)

    waited = False
    for h in (0, 1):
        load_w[h].wait()
        wall[mine, h * 128 : (h + 1) * 128, :] = wf[h * 128 : (h + 1) * 128, :].astype(BF16)
        if not waited:
            pl.semaphore_wait(barrier, len(friends))
            waited = True
        ring(0, 0, h).start()
        ring(1, 0, h).start()
        cross(h, mine).start()

    swap_t = remote(pos_in, pos.at[1], kgs.at[0], kgr.at[0], twin)
    swap_c = remote(cot, cotv.at[1], kgs.at[1], kgr.at[1], twin)
    swap_t.start()
    swap_c.start()

    def load_emb(j):
        b = place(j)
        cols = pl.multiple_of((2 * b + c) * ROWS, ROWS)
        return pltpu.make_async_copy(emb.at[:, pl.ds(cols, ROWS)], emba.at[b, pl.ds(0, TOK)], embl.at[j])

    def swap_emb(j):
        b = place(j)
        cols = pl.multiple_of((2 * b + 1 - c) * ROWS, ROWS)
        return remote(emb.at[:, pl.ds(cols, ROWS)], emba.at[b, pl.ds(TOK, TOK)], embs.at[j], embr.at[j], twin)

    def begin(j, _):
        swap_emb(j).start()
        load_emb(j).start()
        return 0

    lax.fori_loop(0, 16, begin, 0)
    load_p.start()

    lane = lax.broadcasted_iota(jnp.int32, (192, 128), 1)
    low = lane < HD // 2

    def tables(t):
        posf = pos[t].astype(F32)
        cols = [jnp.transpose(jnp.broadcast_to(posf[:, 128 * j : 128 * (j + 1)], (128, 128))) for j in range(3)]
        lower = jnp.concatenate([cols[0], cols[1][:64]], axis=0)
        upper = jnp.concatenate([cols[1][64:], cols[2]], axis=0)
        angle = jnp.where(low, lower, upper) * freq[...]
        cp, sp = jnp.cos(angle), jnp.sin(angle)
        cq, sq = pltpu.roll(cp, 64, 1), pltpu.roll(sp, 64, 1)
        cosv[t, 0:192, :] = jnp.where(low, cp, cq)
        cosv[t, 192:384, :] = jnp.where(low, cq, cp)
        sinv[t, 0:192, :] = jnp.where(low, -sp, sq)
        sinv[t, 192:384, :] = jnp.where(low, -sq, sp)
        return 0

    def back(t):
        for h in range(KV_HEADS):
            u = cotv[t, :, h * HD : (h + 1) * HD].astype(F32)
            g = u * cosv[t] - pltpu.roll(u, 64, 1) * sinv[t]
            kgt[h * HD : (h + 1) * HD, t * TOK : (t + 1) * TOK] = jnp.transpose(g).astype(BF16)

    load_t.wait()
    load_f.wait()
    tables(0)
    load_c.wait()
    back(0)
    swap_t.wait_recv()
    tables(1)
    swap_c.wait_recv()
    back(1)

    def block(j):
        load_emb(j).wait()
        swap_emb(j).wait_recv()
        return jnp.dot(kgt[...], emba[place(j)], preferred_element_type=F32)

    def send_y(i, h):
        rows = pl.ds(pl.multiple_of(h * HALF, HALF), HALF)
        return remote(ysend.at[i, rows], yrecv.at[i, rows], yss.at[i, h], yrr.at[i, h], across)

    def far(i, _):
        ysend[i] = block(i).astype(BF16)
        return 0

    def post_y(i):
        send_y(i, i % 2).start()
        send_y(i, 1 - i % 2).start()

    def next_y(i):
        send_y(i - AHEAD, 0).wait_send()
        send_y(i - AHEAD, 1).wait_send()
        post_y(i)

    def near(i, _):
        own[i] = block(i + 8)
        return 0

    def enter(h):
        cross(h, other).wait_recv()
        for way in (0, 1):
            if travels(way, 1, h):
                ring(way, 1, h).start()

    def advance(k, h):
        for way in (0, 1):
            if travels(way, k, h):
                ring_in(way, k, h).wait_recv()
            if k == 1 and h == 1 and HOP:
                hop(way, 1 - yh).wait_recv()
            if k == 0 and h == 1 and HOP:
                hop(way, yh).start()
            if k + 2 < 8 and travels(way, k + 2, h) and (k < 6):
                ring(way, k + 2, h).start()

    far(0, 0)
    post_y(0)
    far(1, 0)
    post_y(1)
    enter(0)
    advance(0, 0)

    load_p.wait()
    psb[...] = psv[...].astype(BF16)

    def piece(xx):
        return pl.ds(pl.multiple_of(xx * 64, 64), 64)

    stage1 = [
        remote(psb.at[piece(lax.rem(x + k, NX))], p1.at[k - 1], p1ss.at[k - 1], p1rr.at[k - 1], xpeers[k - 1])
        for k in (1, 2, 3)
    ]
    for cp1 in stage1:
        cp1.start()

    far(2, 0)
    lax.fori_loop(3, 5, far, 0)
    enter(1)
    advance(0, 1)
    lax.fori_loop(5, 8, far, 0)
    lax.fori_loop(0, 8, near, 0)
    advance(1, 0)

    def product(b, first=False):
        def part(m, _):
            at = pl.ds(pl.multiple_of(m * 256, 256), 256)
            value = jnp.dot(emba[b, at, :], wall[b], preferred_element_type=F32)
            if first:
                acc[at, :] = value
            else:
                acc[at, :] += value
            return 0

        lax.fori_loop(0, 3, part, 0)

    def products(k):
        d, p = k // 2, k % 2
        plane = yh if p == 0 else 1 - yh
        product(slot(z - d - 1, plane))
        if d < 3:
            product(slot(z + d + 1, plane))

    next_y(2)
    product(mine, True)
    product(other)

    for cp1 in stage1:
        cp1.wait_recv()
    part_sum = psb[piece(x), :].astype(F32)
    for k in range(3):
        part_sum = part_sum + p1[k].astype(F32)
    p2s[...] = part_sum.astype(BF16)
    stage2 = remote(p2s, p2r, p2ss.at[0], p2rr.at[0], ypeer)
    stage2.start()

    def hand(way, step, h):
        rows = pl.ds(h * HALF, HALF)
        return remote(
            zs.at[way, step, rows], zr.at[way, step, rows],
            zss.at[way, step * 2 + h], zrr.at[way, step * 2 + h], nexts[way],
        )

    def here(i, h):
        send_y(i, h).wait_recv()
        rows = pl.ds(h * HALF, HALF)
        return own[i, rows, :] + yrecv[i, rows, :].astype(F32)

    def relay(i, way, step, h):
        rows = pl.ds(h * HALF, HALF)
        total = here(i, h)
        if step > 1 or (step == 1 and h == way):
            hand(way, step - 1, h).wait_recv()
            total = total + zr[way, step - 1, rows, :].astype(F32)
        zs[way, step, rows, :] = total.astype(BF16)
        hand(way, step, h).start()

    next_y(3)
    relay(0, 0, 0, 0)
    relay(0, 1, 0, 1)
    products(0)
    advance(1, 1)
    advance(2, 0)
    advance(2, 1)
    products(1)
    next_y(4)
    relay(1, 0, 1, 1)
    relay(1, 0, 1, 0)

    stage2.wait_recv()
    dsum[piece(x), :] = (p2s[...].astype(F32) + p2r[...].astype(F32)).astype(BF16)

    def stage3(k, home):
        ref = dsum.at[piece(home)]
        return remote(ref, ref, p3ss.at[k - 1], p3rr.at[k - 1], xpeers[k - 1])

    for k in (1, 2, 3):
        stage3(k, x).start()

    products(2)
    advance(3, 0)
    advance(3, 1)
    products(3)
    next_y(5)
    relay(2, 1, 1, 0)
    relay(2, 1, 1, 1)
    advance(4, 0)
    advance(4, 1)
    products(4)
    advance(5, 0)
    advance(5, 1)
    products(5)
    next_y(6)
    relay(3, 0, 2, 1)
    relay(3, 0, 2, 0)
    for k in (1, 2, 3):
        stage3(k, lax.rem(x + NX - k, NX)).wait_recv()
    next_y(7)
    relay(4, 1, 2, 0)
    relay(4, 1, 2, 1)
    advance(6, 0)
    advance(6, 1)
    products(6)
    relay(5, 0, 3, 1)
    relay(5, 0, 3, 0)
    advance(7, 0)
    advance(7, 1)
    products(7)

    give_x = remote(acc.at[pl.ds(TOK, TOK)], accx, xs.at[0], xr.at[0], twin)
    give_x.start()
    relay(6, 1, 3, 0)
    relay(6, 1, 3, 1)
    give_x.wait_recv()
    for h in range(KV_HEADS):
        at = slice(h * HD, (h + 1) * HD)
        plain = acc[0:TOK, at] + accx[:, at]
        keyv[:, at] = (plain * cosv[0] + pltpu.roll(plain, 64, 1) * sinv[0]).astype(BF16)

    for h in (0, 1):
        rows = pl.ds(h * HALF, HALF)
        total = here(7, h)
        for way in (0, 1):
            hand(way, 3, h).wait_recv()
            total = total + zr[way, 3, rows, :].astype(F32)
        gout[:, h * HALF : (h + 1) * HALF] = jnp.transpose(total)

    for h in (0, 1):
        cross(h, mine).wait_send()
        for way in (0, 1):
            for k in range(8):
                if travels(way, k, h):
                    ring(way, k, h).wait_send()
    if HOP:
        for way in (0, 1):
            hop(way, yh).wait_send()
    swap_t.wait_send()
    swap_c.wait_send()
    lax.fori_loop(0, 16, lambda j, _: (swap_emb(j).wait_send(), 0)[1], 0)
    give_x.wait_send()

    def sent(i, _):
        send_y(i, 0).wait_send()
        send_y(i, 1).wait_send()
        return 0

    lax.fori_loop(6, 8, sent, 0)
    for way in (0, 1):
        for step in range(4):
            for h in (0, 1):
                if step > 0 or h == way:
                    hand(way, step, h).wait_send()
    for cp1 in stage1:
        cp1.wait_send()
    stage2.wait_send()
    for k in (1, 2, 3):
        stage3(k, x).wait_send()


def step(embedded, positions, cotangent, weight, pseudo):
    vmem_spec = pl.BlockSpec(memory_space=pltpu.VMEM)
    hbm_spec = pl.BlockSpec(memory_space=pltpu.HBM)
    dma = pltpu.SemaphoreType.DMA
    operands = (embedded, positions, jnp.asarray(frequencies()), cotangent, weight, pseudo)
    return pl.pallas_call(
        kernel,
        out_shape=(
            jax.ShapeDtypeStruct((TOK, KW), BF16),
            jax.ShapeDtypeStruct((ROWS, KW), F32),
            jax.ShapeDtypeStruct((ROWS, KW), BF16),
        ),
        in_specs=[hbm_spec] * 6,
        out_specs=(vmem_spec, vmem_spec, vmem_spec),
        scratch_shapes=[
            pltpu.VMEM((16, 2 * TOK, ROWS), BF16),
            pltpu.VMEM((16, ROWS, KW), BF16),
            pltpu.VMEM((ROWS, KW), F32),
            pltpu.VMEM((2, TOK, KW), BF16),
            pltpu.VMEM((ROWS, KW), F32),
            pltpu.VMEM((ROWS, KW), BF16),
            pltpu.VMEM((KW, 2 * TOK), BF16),
            pltpu.VMEM((8, KW, ROWS), BF16),
            pltpu.VMEM((8, KW, ROWS), BF16),
            pltpu.VMEM((8, KW, ROWS), F32),
            pltpu.VMEM((2, 4, KW, ROWS), BF16),
            pltpu.VMEM((2, 4, KW, ROWS), BF16),
            pltpu.VMEM((2 * TOK, KW), F32),
            pltpu.VMEM((TOK, KW), F32),
            pltpu.VMEM((2, TOK, HD), F32),
            pltpu.VMEM((2, TOK, HD), F32),
            pltpu.VMEM((3, 64, KW), BF16),
            pltpu.VMEM((64, KW), BF16),
            pltpu.VMEM((64, KW), BF16),
            pltpu.VMEM((2, 1, TOK), jnp.int32),
            pltpu.VMEM((1, HD), F32),
            dma((6,)),
            dma((16,)),
            dma((16,)),
            dma((16,)),
            dma((2,)),
            dma((2,)),
            dma((2, 16)),
            dma((2, 16)),
            dma((4,)),
            dma((4,)),
            dma((8, 2)),
            dma((8, 2)),
            dma((2, 8)),
            dma((2, 8)),
            dma((1,)),
            dma((1,)),
            dma((3,)),
            dma((3,)),
            dma((1,)),
            dma((1,)),
            dma((3,)),
            dma((3,)),
        ],
        compiler_params=pltpu.CompilerParams(
            collective_id=0, has_side_effects=True, vmem_limit_bytes=48 * 1024 * 1024
        ),
        cost_estimate=pl.CostEstimate(flops=6442450944, bytes_accessed=10 << 20, transcendentals=0),
    )(*(pltpu.with_memory_space_constraint(v, pltpu.HBM) for v in operands))


def outer_update(delta_sum, count, anchor_rows, momentum_rows):
    mean_delta = delta_sum / count
    momentum_next = 0.9 * momentum_rows + mean_delta
    anchor_next = anchor_rows - 0.7 * (mean_delta + 0.9 * momentum_next)
    return (anchor_next, momentum_next)


def local(
    embedded,
    positions,
    key_cotangent,
    local_weight,
    adam_first,
    adam_second,
    pseudo_grad,
    anchor,
    momentum,
):
    weight = local_weight[0]
    keys, grad, delta = step(embedded[0], positions, key_cotangent[0], weight, pseudo_grad[0])
    first = 0.9 * adam_first[0] + 0.1 * grad
    second = 0.999 * adam_second[0] + 0.001 * grad * grad
    stepped = weight - 0.001 * (first / (jnp.sqrt(second) + 1e-08) + 0.1 * weight)
    replicas = lax.axis_size("replica")
    anchor_next, momentum_next = outer_update(delta.astype(F32), replicas, anchor, momentum)
    merged = 0.5 * anchor_next + 0.5 * stepped
    return (keys[None], merged[None], first[None], second[None], anchor_next, momentum_next)


def solution(mesh):
    return jax.shard_map(
        local,
        mesh=mesh,
        in_specs=(
            P("replica", "fsdp", None),
            P("replica", "fsdp"),
            P("replica", "fsdp", None),
            P("replica", "fsdp", None),
            P("replica", "fsdp", None),
            P("replica", "fsdp", None),
            P("replica", "fsdp", None),
            P("fsdp", None),
            P("fsdp", None),
        ),
        out_specs=(
            P("replica", "fsdp", None),
            P("replica", "fsdp", None),
            P("replica", "fsdp", None),
            P("replica", "fsdp", None),
            P("fsdp", None),
            P("fsdp", None),
        ),
        check_vma=False,
    )
```

```python
import functools
import math

import jax
import jax.numpy as jnp
import numpy as np
from jax import lax
from jax.experimental import pallas as pl
from jax.experimental.pallas import tpu as pltpu
from jax.sharding import PartitionSpec as P

HD = 128
KV_HEADS = 4
NZ = 8
NX = 4
TOK = 384
ROWS = 256
KW = 512
HALF = 256
HOP = 64
AHEAD = 2
MESH = pl.DeviceIdType.MESH
F32 = jnp.float32
BF16 = jnp.bfloat16


def frequencies():
    steps = np.arange(HD // 2, dtype=np.float64)
    freqs = np.exp(steps * (-2.0 * math.log(500000.0) / HD)).astype(np.float32)
    return np.concatenate([freqs, freqs])[None, :]


def kernel(
    emb, pos_in, freq_in, cot, weight, pseudo,
    keyv, gout, dsum,
    emba, wall, wf, cotv, psv, psb, kgt, ysend, yrecv, own, zs, zr, acc, accs, accx,
    cosv, sinv, p1, p2s, p2r, pos, freq,
    loc, embl, embs, embr, kgs, kgr, ags, agr, yas, yar, yss, yrr, zss, zrr, xs, xr, p1ss, p1rr, p2ss, p2rr, p3ss, p3rr,
):
    r = lax.axis_index("replica")
    f = lax.axis_index("fsdp")
    ylo, x = r // NX, r % NX
    z, yh, c = f // 4, (f // 2) % 2, f % 2

    def wrap(v):
        return lax.rem(v + 2 * NZ, NZ)

    def at_z(v):
        return (r, wrap(v) * 4 + yh * 2 + c)

    nexts = (at_z(z + 1), at_z(z - 1))
    across = (r, z * 4 + (1 - yh) * 2 + c)
    twin = (r, z * 4 + yh * 2 + (1 - c))
    xpeers = [(ylo * NX + lax.rem(x + k, NX), f) for k in (1, 2, 3)]
    ypeer = ((1 - ylo) * NX + x, f)

    def remote(src, dst, ss, rs, dev):
        return pltpu.make_async_remote_copy(
            src_ref=src, dst_ref=dst, send_sem=ss, recv_sem=rs, device_id=dev, device_id_type=MESH
        )

    def slot(zz, plane):
        return wrap(zz) * 2 + plane

    def place(j):
        i = j % 8
        away = (4 - (i + 1) // 2) * (2 * (i % 2) - 1)
        return slot(z + away, jnp.where(j < 8, 1 - yh, yh))

    load_w = [
        pltpu.make_async_copy(weight.at[pl.ds(h * 128, 128)], wf.at[pl.ds(h * 128, 128)], loc.at[h]) for h in (0, 1)
    ]
    load_t = pltpu.make_async_copy(pos_in, pos.at[0], loc.at[2])
    load_f = pltpu.make_async_copy(freq_in, freq, loc.at[3])
    load_c = pltpu.make_async_copy(cot, cotv.at[0], loc.at[4])
    load_p = pltpu.make_async_copy(pseudo, psv, loc.at[5])
    load_w[0].start()
    load_w[1].start()
    barrier = pltpu.get_barrier_semaphore()
    friends = [*nexts, across, twin, *xpeers, ypeer]
    for dev in friends:
        pl.semaphore_signal(barrier, inc=1, device_id=dev, device_id_type=MESH)
    load_t.start()
    load_f.start()
    load_c.start()

    mine, other = slot(z, yh), slot(z, 1 - yh)

    def rows_of(k, h):
        if k == 1 and h == 1:
            return pl.ds(128, 128 - HOP)
        return pl.ds(h * 128, 128)

    def travels(way, k, h):
        return h == way if k >= 6 else not (k == 1 and h == 1 and HOP == 128)

    def ring(way, k, h, back=0):
        sign = 1 if way == 0 else -1
        b = slot(z - sign * (k // 2 + back), yh if k % 2 == 0 else 1 - yh)
        ref = wall.at[b, rows_of(k, h)]
        return remote(ref, ref, ags.at[way, k * 2 + h], agr.at[way, k * 2 + h], nexts[way])

    def ring_in(way, k, h):
        return ring(way, k, h, 1)

    def cross(h, b):
        ref = wall.at[b, pl.ds(h * 128, 128)]
        return remote(ref, ref, yas.at[h], yar.at[h], across)

    def hop(way, plane):
        ref = wall.at[slot(z - (1 if way == 0 else -1), plane), pl.ds(ROWS - HOP, HOP)]
        return remote(ref, ref, yas.at[2 + way], yar.at[2 + way], across)

    waited = False
    for h in (0, 1):
        load_w[h].wait()
        wall[mine, h * 128 : (h + 1) * 128, :] = wf[h * 128 : (h + 1) * 128, :].astype(BF16)
        if not waited:
            pl.semaphore_wait(barrier, len(friends))
            waited = True
        ring(0, 0, h).start()
        ring(1, 0, h).start()
        cross(h, mine).start()

    swap_t = remote(pos_in, pos.at[1], kgs.at[0], kgr.at[0], twin)
    swap_c = remote(cot, cotv.at[1], kgs.at[1], kgr.at[1], twin)
    swap_t.start()
    swap_c.start()

    def load_emb(j):
        b = place(j)
        cols = pl.multiple_of((2 * b + c) * ROWS, ROWS)
        return pltpu.make_async_copy(emb.at[:, pl.ds(cols, ROWS)], emba.at[b, pl.ds(0, TOK)], embl.at[j])

    def swap_emb(j):
        b = place(j)
        cols = pl.multiple_of((2 * b + 1 - c) * ROWS, ROWS)
        return remote(emb.at[:, pl.ds(cols, ROWS)], emba.at[b, pl.ds(TOK, TOK)], embs.at[j], embr.at[j], twin)

    def begin_load(j, _):
        load_emb(j).start()
        return 0

    def begin_swap(j, _):
        swap_emb(j).start()
        return 0

    lax.fori_loop(0, 16, begin_load, 0)
    load_p.start()

    lane = lax.broadcasted_iota(jnp.int32, (192, 128), 1)
    low = lane < HD // 2

    def tables(t):
        posf = pos[t].astype(F32)
        cols = [jnp.transpose(jnp.broadcast_to(posf[:, 128 * j : 128 * (j + 1)], (128, 128))) for j in range(3)]
        lower = jnp.concatenate([cols[0], cols[1][:64]], axis=0)
        upper = jnp.concatenate([cols[1][64:], cols[2]], axis=0)
        angle = jnp.where(low, lower, upper) * freq[...]
        cp, sp = jnp.cos(angle), jnp.sin(angle)
        cq, sq = pltpu.roll(cp, 64, 1), pltpu.roll(sp, 64, 1)
        cosv[t, 0:192, :] = jnp.where(low, cp, cq)
        cosv[t, 192:384, :] = jnp.where(low, cq, cp)
        sinv[t, 0:192, :] = jnp.where(low, -sp, sq)
        sinv[t, 192:384, :] = jnp.where(low, -sq, sp)
        return 0

    def back(t):
        for h in range(KV_HEADS):
            u = cotv[t, :, h * HD : (h + 1) * HD].astype(F32)
            g = u * cosv[t] - pltpu.roll(u, 64, 1) * sinv[t]
            kgt[h * HD : (h + 1) * HD, t * TOK : (t + 1) * TOK] = jnp.transpose(g).astype(BF16)

    load_t.wait()
    load_f.wait()
    tables(0)
    load_c.wait()
    back(0)
    lax.fori_loop(0, 2, begin_swap, 0)
    swap_t.wait_recv()
    tables(1)
    swap_c.wait_recv()
    lax.fori_loop(2, 4, begin_swap, 0)
    back(1)

    def block(j):
        load_emb(j).wait()
        swap_emb(j).wait_recv()
        return jnp.dot(kgt[...], emba[place(j)], preferred_element_type=F32)

    def send_y(i, h):
        rows = pl.ds(pl.multiple_of(h * HALF, HALF), HALF)
        return remote(ysend.at[i, rows], yrecv.at[i, rows], yss.at[i, h], yrr.at[i, h], across)

    def far(i, _):
        ysend[i] = block(i).astype(BF16)
        return 0

    def post_y(i):
        send_y(i, i % 2).start()
        send_y(i, 1 - i % 2).start()

    def next_y(i):
        send_y(i - AHEAD, 0).wait_send()
        send_y(i - AHEAD, 1).wait_send()
        post_y(i)

    def near(i, _):
        own[i] = block(i + 8)
        return 0

    def enter(h):
        cross(h, other).wait_recv()
        for way in (0, 1):
            if travels(way, 1, h):
                ring(way, 1, h).start()

    def advance(k, h):
        for way in (0, 1):
            if travels(way, k, h):
                ring_in(way, k, h).wait_recv()
            if k == 1 and h == 1 and HOP:
                hop(way, 1 - yh).wait_recv()
            if k == 0 and h == 1 and HOP:
                hop(way, yh).start()
            if k + 2 < 8 and travels(way, k + 2, h) and (k < 6):
                ring(way, k + 2, h).start()

    far(0, 0)
    post_y(0)
    lax.fori_loop(4, 6, begin_swap, 0)
    far(1, 0)
    post_y(1)
    lax.fori_loop(6, 10, begin_swap, 0)
    enter(0)
    advance(0, 0)

    load_p.wait()
    psb[...] = psv[...].astype(BF16)

    def piece(xx):
        return pl.ds(pl.multiple_of(xx * 64, 64), 64)

    stage1 = [
        remote(psb.at[piece(lax.rem(x + k, NX))], p1.at[k - 1], p1ss.at[k - 1], p1rr.at[k - 1], xpeers[k - 1])
        for k in (1, 2, 3)
    ]
    for cp1 in stage1:
        cp1.start()

    far(2, 0)
    lax.fori_loop(10, 16, begin_swap, 0)
    lax.fori_loop(3, 5, far, 0)
    enter(1)
    advance(0, 1)
    lax.fori_loop(5, 8, far, 0)
    lax.fori_loop(0, 8, near, 0)
    advance(1, 0)

    def product(b, first=False):
        def part(m, _):
            at = pl.ds(pl.multiple_of(m * 256, 256), 256)
            value = jnp.dot(emba[b, at, :], wall[b], preferred_element_type=F32)
            if first:
                acc[at, :] = value
            else:
                acc[at, :] += value
            return 0

        lax.fori_loop(0, 3, part, 0)

    def products(k):
        d, p = k // 2, k % 2
        plane = yh if p == 0 else 1 - yh
        product(slot(z - d - 1, plane))
        if d < 3:
            product(slot(z + d + 1, plane))

    next_y(2)
    product(mine, True)
    product(other)

    for cp1 in stage1:
        cp1.wait_recv()
    part_sum = psb[piece(x), :].astype(F32)
    for k in range(3):
        part_sum = part_sum + p1[k].astype(F32)
    p2s[...] = part_sum.astype(BF16)
    stage2 = remote(p2s, p2r, p2ss.at[0], p2rr.at[0], ypeer)
    stage2.start()

    def hand(way, step, h):
        rows = pl.ds(h * HALF, HALF)
        return remote(
            zs.at[way, step, rows], zr.at[way, step, rows],
            zss.at[way, step * 2 + h], zrr.at[way, step * 2 + h], nexts[way],
        )

    def here(i, h):
        send_y(i, h).wait_recv()
        rows = pl.ds(h * HALF, HALF)
        return own[i, rows, :] + yrecv[i, rows, :].astype(F32)

    def relay(i, way, step, h):
        rows = pl.ds(h * HALF, HALF)
        total = here(i, h)
        if step > 1 or (step == 1 and h == way):
            hand(way, step - 1, h).wait_recv()
            total = total + zr[way, step - 1, rows, :].astype(F32)
        zs[way, step, rows, :] = total.astype(BF16)
        hand(way, step, h).start()

    next_y(3)
    relay(0, 0, 0, 0)
    relay(0, 1, 0, 1)
    products(0)
    advance(1, 1)
    advance(2, 0)
    advance(2, 1)
    products(1)
    next_y(4)
    relay(1, 0, 1, 1)
    relay(1, 0, 1, 0)

    stage2.wait_recv()
    dsum[piece(x), :] = (p2s[...].astype(F32) + p2r[...].astype(F32)).astype(BF16)

    def stage3(k, home):
        ref = dsum.at[piece(home)]
        return remote(ref, ref, p3ss.at[k - 1], p3rr.at[k - 1], xpeers[k - 1])

    for k in (1, 2, 3):
        stage3(k, x).start()

    products(2)
    advance(3, 0)
    advance(3, 1)
    products(3)
    next_y(5)
    relay(2, 1, 1, 0)
    relay(2, 1, 1, 1)
    advance(4, 0)
    advance(4, 1)
    products(4)
    advance(5, 0)
    advance(5, 1)
    products(5)
    next_y(6)
    relay(3, 0, 2, 1)
    relay(3, 0, 2, 0)
    for k in (1, 2, 3):
        stage3(k, lax.rem(x + NX - k, NX)).wait_recv()
    next_y(7)
    relay(4, 1, 2, 0)
    relay(4, 1, 2, 1)
    advance(6, 0)
    advance(6, 1)
    products(6)
    relay(5, 0, 3, 1)
    relay(5, 0, 3, 0)
    relay(6, 1, 3, 0)
    relay(6, 1, 3, 1)
    advance(7, 0)
    advance(7, 1)
    products(7)

    accs[...] = acc[TOK : 2 * TOK, :].astype(BF16)
    give_x = remote(accs, accx, xs.at[0], xr.at[0], twin)
    give_x.start()
    for h in (0, 1):
        rows = pl.ds(h * HALF, HALF)
        total = here(7, h)
        for way in (0, 1):
            hand(way, 3, h).wait_recv()
            total = total + zr[way, 3, rows, :].astype(F32)
        gout[:, h * HALF : (h + 1) * HALF] = jnp.transpose(total)

    give_x.wait_recv()
    for h in range(KV_HEADS):
        at = slice(h * HD, (h + 1) * HD)
        plain = acc[0:TOK, at] + accx[:, at].astype(F32)
        keyv[:, at] = (plain * cosv[0] + pltpu.roll(plain, 64, 1) * sinv[0]).astype(BF16)

    for h in (0, 1):
        cross(h, mine).wait_send()
        for way in (0, 1):
            for k in range(8):
                if travels(way, k, h):
                    ring(way, k, h).wait_send()
    if HOP:
        for way in (0, 1):
            hop(way, yh).wait_send()
    swap_t.wait_send()
    swap_c.wait_send()
    lax.fori_loop(0, 16, lambda j, _: (swap_emb(j).wait_send(), 0)[1], 0)
    give_x.wait_send()

    def sent(i, _):
        send_y(i, 0).wait_send()
        send_y(i, 1).wait_send()
        return 0

    lax.fori_loop(6, 8, sent, 0)
    for way in (0, 1):
        for step in range(4):
            for h in (0, 1):
                if step > 0 or h == way:
                    hand(way, step, h).wait_send()
    for cp1 in stage1:
        cp1.wait_send()
    stage2.wait_send()
    for k in (1, 2, 3):
        stage3(k, x).wait_send()


def step(embedded, positions, cotangent, weight, pseudo):
    vmem_spec = pl.BlockSpec(memory_space=pltpu.VMEM)
    hbm_spec = pl.BlockSpec(memory_space=pltpu.HBM)
    dma = pltpu.SemaphoreType.DMA
    operands = (embedded, positions, jnp.asarray(frequencies()), cotangent, weight, pseudo)
    return pl.pallas_call(
        kernel,
        out_shape=(
            jax.ShapeDtypeStruct((TOK, KW), BF16),
            jax.ShapeDtypeStruct((ROWS, KW), F32),
            jax.ShapeDtypeStruct((ROWS, KW), BF16),
        ),
        in_specs=[hbm_spec] * 6,
        out_specs=(vmem_spec, vmem_spec, vmem_spec),
        scratch_shapes=[
            pltpu.VMEM((16, 2 * TOK, ROWS), BF16),
            pltpu.VMEM((16, ROWS, KW), BF16),
            pltpu.VMEM((ROWS, KW), F32),
            pltpu.VMEM((2, TOK, KW), BF16),
            pltpu.VMEM((ROWS, KW), F32),
            pltpu.VMEM((ROWS, KW), BF16),
            pltpu.VMEM((KW, 2 * TOK), BF16),
            pltpu.VMEM((8, KW, ROWS), BF16),
            pltpu.VMEM((8, KW, ROWS), BF16),
            pltpu.VMEM((8, KW, ROWS), F32),
            pltpu.VMEM((2, 4, KW, ROWS), BF16),
            pltpu.VMEM((2, 4, KW, ROWS), BF16),
            pltpu.VMEM((2 * TOK, KW), F32),
            pltpu.VMEM((TOK, KW), BF16),
            pltpu.VMEM((TOK, KW), BF16),
            pltpu.VMEM((2, TOK, HD), F32),
            pltpu.VMEM((2, TOK, HD), F32),
            pltpu.VMEM((3, 64, KW), BF16),
            pltpu.VMEM((64, KW), BF16),
            pltpu.VMEM((64, KW), BF16),
            pltpu.VMEM((2, 1, TOK), jnp.int32),
            pltpu.VMEM((1, HD), F32),
            dma((6,)),
            dma((16,)),
            dma((16,)),
            dma((16,)),
            dma((2,)),
            dma((2,)),
            dma((2, 16)),
            dma((2, 16)),
            dma((4,)),
            dma((4,)),
            dma((8, 2)),
            dma((8, 2)),
            dma((2, 8)),
            dma((2, 8)),
            dma((1,)),
            dma((1,)),
            dma((3,)),
            dma((3,)),
            dma((1,)),
            dma((1,)),
            dma((3,)),
            dma((3,)),
        ],
        compiler_params=pltpu.CompilerParams(
            collective_id=0, has_side_effects=True, vmem_limit_bytes=48 * 1024 * 1024
        ),
        cost_estimate=pl.CostEstimate(flops=6442450944, bytes_accessed=10 << 20, transcendentals=0),
    )(*(pltpu.with_memory_space_constraint(v, pltpu.HBM) for v in operands))


def finish_kernel(
    grad, delta, keys, weight, first, second, anchor, momentum,
    keys_out, merged_out, first_out, second_out, anchor_out, momentum_out,
    merged_v, first_v, second_v, anchor_v, momentum_v, sems,
):
    save_k = pltpu.make_async_copy(keys, keys_out, sems.at[0])
    save_k.start()
    saves = [save_k]

    def save(src, dst, h):
        rows = pl.ds(h * 128, 128)
        copy = pltpu.make_async_copy(src.at[rows], dst.at[rows], sems.at[len(saves)])
        copy.start()
        saves.append(copy)

    for h in (0, 1):
        at = slice(h * 128, (h + 1) * 128)
        mean_delta = delta[at, :].astype(F32) / 8
        momentum_next = 0.9 * momentum[at, :] + mean_delta
        anchor_next = anchor[at, :] - 0.7 * (mean_delta + 0.9 * momentum_next)
        momentum_v[at, :] = momentum_next
        anchor_v[at, :] = anchor_next
        save(momentum_v, momentum_out, h)
        save(anchor_v, anchor_out, h)
        slope = grad[at, :]
        first_next = 0.9 * first[at, :] + 0.1 * slope
        second_next = 0.999 * second[at, :] + 0.001 * slope * slope
        first_v[at, :] = first_next
        second_v[at, :] = second_next
        save(first_v, first_out, h)
        save(second_v, second_out, h)
        held = weight[at, :]
        stepped = held - 0.001 * (first_next / (jnp.sqrt(second_next) + 1e-08) + 0.1 * held)
        merged_v[at, :] = 0.5 * anchor_next + 0.5 * stepped
        save(merged_v, merged_out, h)
    for copy in saves:
        copy.wait()


def finish(*operands):
    vmem_spec = pl.BlockSpec(memory_space=pltpu.VMEM)
    any_spec = pl.BlockSpec(memory_space=pl.ANY)
    block = jax.ShapeDtypeStruct((ROWS, KW), F32)
    return pl.pallas_call(
        finish_kernel,
        out_shape=(jax.ShapeDtypeStruct((TOK, KW), BF16), *[block] * 5),
        in_specs=[vmem_spec] * 8,
        out_specs=(any_spec,) * 6,
        scratch_shapes=[*[pltpu.VMEM((ROWS, KW), F32)] * 5, pltpu.SemaphoreType.DMA((11,))],
        compiler_params=pltpu.CompilerParams(vmem_limit_bytes=8 * 1024 * 1024),
        cost_estimate=pl.CostEstimate(flops=4 << 20, bytes_accessed=6 << 20, transcendentals=0),
    )(*operands)


def local(
    embedded,
    positions,
    key_cotangent,
    local_weight,
    adam_first,
    adam_second,
    pseudo_grad,
    anchor,
    momentum,
):
    weight = local_weight[0]
    keys, grad, delta = step(embedded[0], positions, key_cotangent[0], weight, pseudo_grad[0])
    keys, merged, first, second, anchor_next, momentum_next = finish(
        grad, delta, keys, weight, adam_first[0], adam_second[0], anchor, momentum
    )
    return (keys[None], merged[None], first[None], second[None], anchor_next, momentum_next)


def solution(mesh):
    return jax.shard_map(
        local,
        mesh=mesh,
        in_specs=(
            P("replica", "fsdp", None),
            P("replica", "fsdp"),
            P("replica", "fsdp", None),
            P("replica", "fsdp", None),
            P("replica", "fsdp", None),
            P("replica", "fsdp", None),
            P("replica", "fsdp", None),
            P("fsdp", None),
            P("fsdp", None),
        ),
        out_specs=(
            P("replica", "fsdp", None),
            P("replica", "fsdp", None),
            P("replica", "fsdp", None),
            P("replica", "fsdp", None),
            P("fsdp", None),
            P("fsdp", None),
        ),
        check_vma=False,
    )
```

```python
import functools
import math

import jax
import jax.numpy as jnp
import numpy as np
from jax import lax
from jax.experimental import pallas as pl
from jax.experimental.pallas import tpu as pltpu
from jax.sharding import PartitionSpec as P

HD = 128
KV_HEADS = 4
NZ = 8
NX = 4
TOK = 384
ROWS = 256
KW = 512
HALF = 256
HOP = 48
AHEAD = 2
MESH = pl.DeviceIdType.MESH
F32 = jnp.float32
BF16 = jnp.bfloat16


def frequencies():
    steps = np.arange(HD // 2, dtype=np.float64)
    freqs = np.exp(steps * (-2.0 * math.log(500000.0) / HD)).astype(np.float32)
    return np.concatenate([freqs, freqs])[None, :]


def kernel(
    emb, pos_in, freq_in, cot, weight, pseudo,
    keyv, gout, dsum,
    emba, wall, wf, cotv, psv, psb, kgt, ysend, yrecv, own, zs, zr, acc, accs, accx,
    cosv, sinv, p1, p2s, p2r, pos, freq,
    loc, embl, embs, embr, kgs, kgr, ags, agr, yas, yar, yss, yrr, zss, zrr, xs, xr, p1ss, p1rr, p2ss, p2rr, p3ss, p3rr,
):
    r = lax.axis_index("replica")
    f = lax.axis_index("fsdp")
    ylo, x = r // NX, r % NX
    z, yh, c = f // 4, (f // 2) % 2, f % 2

    def wrap(v):
        return lax.rem(v + 2 * NZ, NZ)

    def at_z(v):
        return (r, wrap(v) * 4 + yh * 2 + c)

    nexts = (at_z(z + 1), at_z(z - 1))
    across = (r, z * 4 + (1 - yh) * 2 + c)
    twin = (r, z * 4 + yh * 2 + (1 - c))
    xpeers = [(ylo * NX + lax.rem(x + k, NX), f) for k in (1, 2, 3)]
    ypeer = ((1 - ylo) * NX + x, f)

    def remote(src, dst, ss, rs, dev):
        return pltpu.make_async_remote_copy(
            src_ref=src, dst_ref=dst, send_sem=ss, recv_sem=rs, device_id=dev, device_id_type=MESH
        )

    def slot(zz, plane):
        return wrap(zz) * 2 + plane

    def place(j):
        i = j % 8
        away = (4 - (i + 1) // 2) * (2 * (i % 2) - 1)
        return slot(z + away, jnp.where(j < 8, 1 - yh, yh))

    load_w = [
        pltpu.make_async_copy(weight.at[pl.ds(h * 128, 128)], wf.at[pl.ds(h * 128, 128)], loc.at[h]) for h in (0, 1)
    ]
    load_t = pltpu.make_async_copy(pos_in, pos.at[0], loc.at[2])
    load_f = pltpu.make_async_copy(freq_in, freq, loc.at[3])
    load_c = pltpu.make_async_copy(cot, cotv.at[0], loc.at[4])
    load_p = pltpu.make_async_copy(pseudo, psv, loc.at[5])
    load_w[0].start()
    load_w[1].start()
    barrier = pltpu.get_barrier_semaphore()
    friends = [*nexts, across, twin, *xpeers, ypeer]
    for dev in friends:
        pl.semaphore_signal(barrier, inc=1, device_id=dev, device_id_type=MESH)
    load_t.start()
    load_f.start()
    load_c.start()

    mine, other = slot(z, yh), slot(z, 1 - yh)

    def rows_of(k, h):
        if k == 1 and h == 1:
            return pl.ds(128, 128 - HOP)
        return pl.ds(h * 128, 128)

    def travels(way, k, h):
        return h == way if k >= 6 else not (k == 1 and h == 1 and HOP == 128)

    def ring(way, k, h, back=0):
        sign = 1 if way == 0 else -1
        b = slot(z - sign * (k // 2 + back), yh if k % 2 == 0 else 1 - yh)
        ref = wall.at[b, rows_of(k, h)]
        return remote(ref, ref, ags.at[way, k * 2 + h], agr.at[way, k * 2 + h], nexts[way])

    def ring_in(way, k, h):
        return ring(way, k, h, 1)

    def cross(h, b):
        ref = wall.at[b, pl.ds(h * 128, 128)]
        return remote(ref, ref, yas.at[h], yar.at[h], across)

    def hop(way, plane):
        ref = wall.at[slot(z - (1 if way == 0 else -1), plane), pl.ds(ROWS - HOP, HOP)]
        return remote(ref, ref, yas.at[2 + way], yar.at[2 + way], across)

    waited = False
    for h in (0, 1):
        load_w[h].wait()
        wall[mine, h * 128 : (h + 1) * 128, :] = wf[h * 128 : (h + 1) * 128, :].astype(BF16)
        if not waited:
            pl.semaphore_wait(barrier, len(friends))
            waited = True
        ring(0, 0, h).start()
        ring(1, 0, h).start()
        cross(h, mine).start()

    swap_t = remote(pos_in, pos.at[1], kgs.at[0], kgr.at[0], twin)
    swap_c = remote(cot, cotv.at[1], kgs.at[1], kgr.at[1], twin)
    swap_t.start()
    swap_c.start()

    def load_emb(j):
        b = place(j)
        cols = pl.multiple_of((2 * b + c) * ROWS, ROWS)
        return pltpu.make_async_copy(emb.at[:, pl.ds(cols, ROWS)], emba.at[b, pl.ds(0, TOK)], embl.at[j])

    def swap_emb(j):
        b = place(j)
        cols = pl.multiple_of((2 * b + 1 - c) * ROWS, ROWS)
        return remote(emb.at[:, pl.ds(cols, ROWS)], emba.at[b, pl.ds(TOK, TOK)], embs.at[j], embr.at[j], twin)

    def begin_load(j, _):
        load_emb(j).start()
        return 0

    def begin_swap(j, _):
        swap_emb(j).start()
        return 0

    lax.fori_loop(0, 16, begin_load, 0)
    load_p.start()

    lane = lax.broadcasted_iota(jnp.int32, (192, 128), 1)
    low = lane < HD // 2

    def tables(t):
        posf = pos[t].astype(F32)
        cols = [jnp.transpose(jnp.broadcast_to(posf[:, 128 * j : 128 * (j + 1)], (128, 128))) for j in range(3)]
        lower = jnp.concatenate([cols[0], cols[1][:64]], axis=0)
        upper = jnp.concatenate([cols[1][64:], cols[2]], axis=0)
        angle = jnp.where(low, lower, upper) * freq[...]
        cp, sp = jnp.cos(angle), jnp.sin(angle)
        cq, sq = pltpu.roll(cp, 64, 1), pltpu.roll(sp, 64, 1)
        cosv[t, 0:192, :] = jnp.where(low, cp, cq)
        cosv[t, 192:384, :] = jnp.where(low, cq, cp)
        sinv[t, 0:192, :] = jnp.where(low, -sp, sq)
        sinv[t, 192:384, :] = jnp.where(low, -sq, sp)
        return 0

    def back(t):
        for h in range(KV_HEADS):
            u = cotv[t, :, h * HD : (h + 1) * HD].astype(F32)
            g = u * cosv[t] - pltpu.roll(u, 64, 1) * sinv[t]
            kgt[h * HD : (h + 1) * HD, t * TOK : (t + 1) * TOK] = jnp.transpose(g).astype(BF16)

    load_t.wait()
    load_f.wait()
    tables(0)
    load_c.wait()
    back(0)
    lax.fori_loop(0, 2, begin_swap, 0)
    swap_t.wait_recv()
    tables(1)
    swap_c.wait_recv()
    lax.fori_loop(2, 4, begin_swap, 0)
    back(1)

    def block(j):
        load_emb(j).wait()
        swap_emb(j).wait_recv()
        return jnp.dot(kgt[...], emba[place(j)], preferred_element_type=F32)

    def send_y(i, h):
        rows = pl.ds(pl.multiple_of(h * HALF, HALF), HALF)
        return remote(ysend.at[i, rows], yrecv.at[i, rows], yss.at[i, h], yrr.at[i, h], across)

    def far(i, _):
        ysend[i] = block(i).astype(BF16)
        return 0

    def post_y(i):
        send_y(i, i % 2).start()
        send_y(i, 1 - i % 2).start()

    def next_y(i):
        send_y(i - AHEAD, 0).wait_send()
        send_y(i - AHEAD, 1).wait_send()
        post_y(i)

    def near(i, _):
        own[i] = block(i + 8)
        return 0

    def enter(h):
        cross(h, other).wait_recv()
        for way in (0, 1):
            if travels(way, 1, h):
                ring(way, 1, h).start()

    def advance(k, h):
        for way in (0, 1):
            if travels(way, k, h):
                ring_in(way, k, h).wait_recv()
            if k == 1 and h == 1 and HOP:
                hop(way, 1 - yh).wait_recv()
            if k == 0 and h == 1 and HOP:
                hop(way, yh).start()
            if k + 2 < 8 and travels(way, k + 2, h) and (k < 6):
                ring(way, k + 2, h).start()

    far(0, 0)
    post_y(0)
    lax.fori_loop(4, 6, begin_swap, 0)
    far(1, 0)
    post_y(1)
    lax.fori_loop(6, 10, begin_swap, 0)
    enter(0)
    advance(0, 0)

    load_p.wait()
    psb[...] = psv[...].astype(BF16)

    def piece(xx):
        return pl.ds(pl.multiple_of(xx * 64, 64), 64)

    stage1 = [
        remote(psb.at[piece(lax.rem(x + k, NX))], p1.at[k - 1], p1ss.at[k - 1], p1rr.at[k - 1], xpeers[k - 1])
        for k in (1, 2, 3)
    ]
    for cp1 in stage1:
        cp1.start()

    far(2, 0)
    lax.fori_loop(10, 16, begin_swap, 0)
    lax.fori_loop(3, 5, far, 0)
    enter(1)
    advance(0, 1)
    lax.fori_loop(5, 8, far, 0)
    lax.fori_loop(0, 8, near, 0)
    advance(1, 0)

    def product(b, first=False, begin=0, end=3):
        def part(m, _):
            at = pl.ds(pl.multiple_of(m * 256, 256), 256)
            value = jnp.dot(emba[b, at, :], wall[b], preferred_element_type=F32)
            if first:
                acc[at, :] = value
            else:
                acc[at, :] += value
            return 0

        lax.fori_loop(begin, end, part, 0)

    def products(k):
        d, p = k // 2, k % 2
        plane = yh if p == 0 else 1 - yh
        product(slot(z - d - 1, plane))
        if d < 3:
            product(slot(z + d + 1, plane))

    next_y(2)
    product(mine, True)
    product(other)

    for cp1 in stage1:
        cp1.wait_recv()
    part_sum = psb[piece(x), :].astype(F32)
    for k in range(3):
        part_sum = part_sum + p1[k].astype(F32)
    p2s[...] = part_sum.astype(BF16)
    stage2 = remote(p2s, p2r, p2ss.at[0], p2rr.at[0], ypeer)
    stage2.start()

    def hand(way, step, h):
        rows = pl.ds(h * HALF, HALF)
        return remote(
            zs.at[way, step, rows], zr.at[way, step, rows],
            zss.at[way, step * 2 + h], zrr.at[way, step * 2 + h], nexts[way],
        )

    def here(i, h):
        send_y(i, h).wait_recv()
        rows = pl.ds(h * HALF, HALF)
        return own[i, rows, :] + yrecv[i, rows, :].astype(F32)

    def relay(i, way, step, h):
        rows = pl.ds(h * HALF, HALF)
        total = here(i, h)
        if step > 1 or (step == 1 and h == way):
            hand(way, step - 1, h).wait_recv()
            total = total + zr[way, step - 1, rows, :].astype(F32)
        zs[way, step, rows, :] = total.astype(BF16)
        hand(way, step, h).start()

    next_y(3)
    relay(0, 0, 0, 0)
    relay(0, 1, 0, 1)
    products(0)
    advance(1, 1)
    advance(2, 0)
    advance(2, 1)
    products(1)
    next_y(4)
    relay(1, 0, 1, 1)
    relay(1, 0, 1, 0)

    stage2.wait_recv()
    dsum[piece(x), :] = (p2s[...].astype(F32) + p2r[...].astype(F32)).astype(BF16)

    def stage3(k, home):
        ref = dsum.at[piece(home)]
        return remote(ref, ref, p3ss.at[k - 1], p3rr.at[k - 1], xpeers[k - 1])

    for k in (1, 2, 3):
        stage3(k, x).start()

    products(2)
    advance(3, 0)
    advance(3, 1)
    products(3)
    next_y(5)
    relay(2, 1, 1, 0)
    relay(2, 1, 1, 1)
    advance(4, 0)
    advance(4, 1)
    products(4)
    advance(5, 0)
    advance(5, 1)
    products(5)
    next_y(6)
    relay(3, 0, 2, 1)
    relay(3, 0, 2, 0)
    for k in (1, 2, 3):
        stage3(k, lax.rem(x + NX - k, NX)).wait_recv()
    next_y(7)
    relay(4, 1, 2, 0)
    relay(4, 1, 2, 1)
    advance(6, 0)
    advance(6, 1)
    products(6)
    relay(5, 0, 3, 1)
    relay(5, 0, 3, 0)
    relay(6, 1, 3, 0)
    relay(6, 1, 3, 1)
    advance(7, 0)
    advance(7, 1)
    product(slot(z - 4, 1 - yh), begin=1)

    accs[...] = acc[TOK : 2 * TOK, :].astype(BF16)
    give_x = remote(accs, accx, xs.at[0], xr.at[0], twin)
    give_x.start()
    product(slot(z - 4, 1 - yh), end=1)
    for h in (0, 1):
        rows = pl.ds(h * HALF, HALF)
        total = here(7, h)
        for way in (0, 1):
            hand(way, 3, h).wait_recv()
            total = total + zr[way, 3, rows, :].astype(F32)
        gout[:, h * HALF : (h + 1) * HALF] = jnp.transpose(total)

    give_x.wait_recv()
    for h in range(KV_HEADS):
        at = slice(h * HD, (h + 1) * HD)
        plain = acc[0:TOK, at] + accx[:, at].astype(F32)
        keyv[:, at] = (plain * cosv[0] + pltpu.roll(plain, 64, 1) * sinv[0]).astype(BF16)

    for h in (0, 1):
        cross(h, mine).wait_send()
        for way in (0, 1):
            for k in range(8):
                if travels(way, k, h):
                    ring(way, k, h).wait_send()
    if HOP:
        for way in (0, 1):
            hop(way, yh).wait_send()
    swap_t.wait_send()
    swap_c.wait_send()
    lax.fori_loop(0, 16, lambda j, _: (swap_emb(j).wait_send(), 0)[1], 0)
    give_x.wait_send()

    def sent(i, _):
        send_y(i, 0).wait_send()
        send_y(i, 1).wait_send()
        return 0

    lax.fori_loop(6, 8, sent, 0)
    for way in (0, 1):
        for step in range(4):
            for h in (0, 1):
                if step > 0 or h == way:
                    hand(way, step, h).wait_send()
    for cp1 in stage1:
        cp1.wait_send()
    stage2.wait_send()
    for k in (1, 2, 3):
        stage3(k, x).wait_send()


def step(embedded, positions, cotangent, weight, pseudo):
    vmem_spec = pl.BlockSpec(memory_space=pltpu.VMEM)
    hbm_spec = pl.BlockSpec(memory_space=pltpu.HBM)
    dma = pltpu.SemaphoreType.DMA
    operands = (embedded, positions, jnp.asarray(frequencies()), cotangent, weight, pseudo)
    return pl.pallas_call(
        kernel,
        out_shape=(
            jax.ShapeDtypeStruct((TOK, KW), BF16),
            jax.ShapeDtypeStruct((ROWS, KW), F32),
            jax.ShapeDtypeStruct((ROWS, KW), BF16),
        ),
        in_specs=[hbm_spec] * 6,
        out_specs=(vmem_spec, vmem_spec, vmem_spec),
        scratch_shapes=[
            pltpu.VMEM((16, 2 * TOK, ROWS), BF16),
            pltpu.VMEM((16, ROWS, KW), BF16),
            pltpu.VMEM((ROWS, KW), F32),
            pltpu.VMEM((2, TOK, KW), BF16),
            pltpu.VMEM((ROWS, KW), F32),
            pltpu.VMEM((ROWS, KW), BF16),
            pltpu.VMEM((KW, 2 * TOK), BF16),
            pltpu.VMEM((8, KW, ROWS), BF16),
            pltpu.VMEM((8, KW, ROWS), BF16),
            pltpu.VMEM((8, KW, ROWS), F32),
            pltpu.VMEM((2, 4, KW, ROWS), BF16),
            pltpu.VMEM((2, 4, KW, ROWS), BF16),
            pltpu.VMEM((2 * TOK, KW), F32),
            pltpu.VMEM((TOK, KW), BF16),
            pltpu.VMEM((TOK, KW), BF16),
            pltpu.VMEM((2, TOK, HD), F32),
            pltpu.VMEM((2, TOK, HD), F32),
            pltpu.VMEM((3, 64, KW), BF16),
            pltpu.VMEM((64, KW), BF16),
            pltpu.VMEM((64, KW), BF16),
            pltpu.VMEM((2, 1, TOK), jnp.int32),
            pltpu.VMEM((1, HD), F32),
            dma((6,)),
            dma((16,)),
            dma((16,)),
            dma((16,)),
            dma((2,)),
            dma((2,)),
            dma((2, 16)),
            dma((2, 16)),
            dma((4,)),
            dma((4,)),
            dma((8, 2)),
            dma((8, 2)),
            dma((2, 8)),
            dma((2, 8)),
            dma((1,)),
            dma((1,)),
            dma((3,)),
            dma((3,)),
            dma((1,)),
            dma((1,)),
            dma((3,)),
            dma((3,)),
        ],
        compiler_params=pltpu.CompilerParams(
            collective_id=0, has_side_effects=True, vmem_limit_bytes=48 * 1024 * 1024
        ),
        cost_estimate=pl.CostEstimate(flops=6442450944, bytes_accessed=10 << 20, transcendentals=0),
    )(*(pltpu.with_memory_space_constraint(v, pltpu.HBM) for v in operands))


def finish_kernel(
    grad, delta, keys, weight, first, second, anchor, momentum,
    keys_out, merged_out, first_out, second_out, anchor_out, momentum_out,
    merged_v, first_v, second_v, anchor_v, momentum_v, sems,
):
    save_k = pltpu.make_async_copy(keys, keys_out, sems.at[0])
    save_k.start()
    saves = [save_k]

    def save(src, dst, h):
        rows = pl.ds(h * 128, 128)
        copy = pltpu.make_async_copy(src.at[rows], dst.at[rows], sems.at[len(saves)])
        copy.start()
        saves.append(copy)

    for h in (0, 1):
        at = slice(h * 128, (h + 1) * 128)
        mean_delta = delta[at, :].astype(F32) / 8
        momentum_next = 0.9 * momentum[at, :] + mean_delta
        anchor_next = anchor[at, :] - 0.7 * (mean_delta + 0.9 * momentum_next)
        momentum_v[at, :] = momentum_next
        anchor_v[at, :] = anchor_next
        save(momentum_v, momentum_out, h)
        save(anchor_v, anchor_out, h)
        slope = grad[at, :]
        first_next = 0.9 * first[at, :] + 0.1 * slope
        second_next = 0.999 * second[at, :] + 0.001 * slope * slope
        first_v[at, :] = first_next
        second_v[at, :] = second_next
        save(first_v, first_out, h)
        save(second_v, second_out, h)
        held = weight[at, :]
        stepped = held - 0.001 * (first_next / (jnp.sqrt(second_next) + 1e-08) + 0.1 * held)
        merged_v[at, :] = 0.5 * anchor_next + 0.5 * stepped
        save(merged_v, merged_out, h)
    for copy in saves:
        copy.wait()


def finish(*operands):
    vmem_spec = pl.BlockSpec(memory_space=pltpu.VMEM)
    any_spec = pl.BlockSpec(memory_space=pl.ANY)
    block = jax.ShapeDtypeStruct((ROWS, KW), F32)
    return pl.pallas_call(
        finish_kernel,
        out_shape=(jax.ShapeDtypeStruct((TOK, KW), BF16), *[block] * 5),
        in_specs=[vmem_spec] * 8,
        out_specs=(any_spec,) * 6,
        scratch_shapes=[*[pltpu.VMEM((ROWS, KW), F32)] * 5, pltpu.SemaphoreType.DMA((11,))],
        compiler_params=pltpu.CompilerParams(vmem_limit_bytes=8 * 1024 * 1024),
        cost_estimate=pl.CostEstimate(flops=4 << 20, bytes_accessed=6 << 20, transcendentals=0),
    )(*operands)


def local(
    embedded,
    positions,
    key_cotangent,
    local_weight,
    adam_first,
    adam_second,
    pseudo_grad,
    anchor,
    momentum,
):
    weight = local_weight[0]
    keys, grad, delta = step(embedded[0], positions, key_cotangent[0], weight, pseudo_grad[0])
    keys, merged, first, second, anchor_next, momentum_next = finish(
        grad, delta, keys, weight, adam_first[0], adam_second[0], anchor, momentum
    )
    return (keys[None], merged[None], first[None], second[None], anchor_next, momentum_next)


def solution(mesh):
    return jax.shard_map(
        local,
        mesh=mesh,
        in_specs=(
            P("replica", "fsdp", None),
            P("replica", "fsdp"),
            P("replica", "fsdp", None),
            P("replica", "fsdp", None),
            P("replica", "fsdp", None),
            P("replica", "fsdp", None),
            P("replica", "fsdp", None),
            P("fsdp", None),
            P("fsdp", None),
        ),
        out_specs=(
            P("replica", "fsdp", None),
            P("replica", "fsdp", None),
            P("replica", "fsdp", None),
            P("replica", "fsdp", None),
            P("fsdp", None),
            P("fsdp", None),
        ),
        check_vma=False,
    )
```
